32 devices in a mesh: ctx: 8 (over z, x), head: 4 (over y, core).
Axes of the slice: x: 2, y: 2, z: 4, core: 2. Of those that a mesh axis runs over, the one named last changes fastest.
Arguments:
- inputs: bfloat16 [8192, 2048], P('ctx', 'head'), may hold values from -6 to 6
- level_factors: float32 [16, 13, 8192], P('head', None, 'ctx'), may hold values from 0.1 to 1
- out_grad: bfloat16 [8192, 2048], P('ctx', 'head'), may hold values from -6 to 6
- master: float32 [3, 2048, 2048], P(None, 'ctx', 'head'), may hold values from -0.125 to 0.125
- moment_one: float32 [3, 2048, 2048], P(None, 'ctx', 'head'), may hold values from -0.024 to 0.024
- moment_two: float32 [3, 2048, 2048], P(None, 'ctx', 'head'), may hold values from 1e-06 to 0.0001
Outputs:
- attention: bfloat16 [8192, 2048], P('ctx', 'head')
- new_weights: bfloat16 [3, 2048, 2048], P(None, None, 'head')
The draws below stay inside these ranges and needn't reach their ends.
All inputs are finite; a program needn't handle non-finite values.
Results may differ from the reference program's by a relative error of at most 0.0033.
The reference program's roundings to bfloat16 on the way count: a program that leaves them out, or rounds other values in their place, can miss the bound.
Values may be sent and summed in bfloat16 or wider, within the bound.
A program may use at most 128 MiB of HBM per device.

```python
import math
import jax
import jax.numpy as jnp
from jax import lax

D = 2048
H = 16
DH = 128
LV_IN = 8
LV_OUT = 5
TOK_DEV = 1024
TOKENS = 8192
LEVELS = 13


def block_scale(rng, extent, pieces, smallest, high):
    gain, own = 1.0, jax.random.fold_in(rng, 6)
    for position, blocks in pieces:
        steps = jnp.exp(jax.random.uniform(jax.random.fold_in(own, position), (blocks,), jnp.float32, smallest / len(pieces), high / len(pieces)))
        gain = gain * jnp.repeat(steps, extent[position] // blocks).reshape([-1 if axis == position else 1 for axis in range(len(extent))])
    return gain


def scatter_about(rng, dims, spread, reach, split=(), kind=jnp.bfloat16):
    array = jax.random.normal(rng, dims, jnp.float32) * spread
    if len(split) > 0:
        array = block_scale(rng, dims, split, -0.22, 0.18) * array
    return jnp.clip(array, min=-reach, max=reach).astype(kind)


def setup_inputs(seed: int = 0) -> dict:
    arg_keys = jax.random.split(jax.random.key(seed), 7)
    inputs = scatter_about(arg_keys[0], (TOKENS, D), 1.0, 6.0, ((0, 8), (1, 4)))
    level_factors = jnp.clip(jnp.exp(math.log(1.0) - 2.3025851 * jax.random.uniform(arg_keys[1], (H, LEVELS, TOKENS), jnp.float32) ** block_scale(arg_keys[1], (H, LEVELS, TOKENS), ((0, 4), (2, 8)), -0.2, 0.2)), 0.1, 1.0)
    out_grad = scatter_about(arg_keys[2], (TOKENS, H * DH), 1.0, 6.0, ((0, 8), (1, 4)))
    master = scatter_about(arg_keys[3], (3, D, H * DH), D ** -0.5, 0.125, ((1, 8), (2, 4)), jnp.float32)
    moment_one = scatter_about(arg_keys[4], (3, D, H * DH), 0.004, 0.024, ((1, 8), (2, 4)), jnp.float32)
    moment_two = jnp.clip(jnp.exp(math.log(0.0001) - 4.6051702 * jax.random.uniform(arg_keys[5], (3, D, H * DH), jnp.float32) ** block_scale(arg_keys[5], (3, D, H * DH), ((1, 8), (2, 4)), -0.2, 0.2)), 9.999999974752427e-07, 0.0001)
    return {"inputs": inputs, "level_factors": level_factors, "out_grad": out_grad, "master": master, "moment_one": moment_one, "moment_two": moment_two}


PRECISE = lax.Precision.HIGHEST

def inner_weights(factors_in):
    rows_count = factors_in.shape[2]
    row_pos = lax.broadcasted_iota(jnp.int32, (rows_count, rows_count), 0)
    col_pos = lax.broadcasted_iota(jnp.int32, (rows_count, rows_count), 1)
    crossed = jnp.bitwise_xor(row_pos, col_pos)
    levels = jnp.zeros(crossed.shape, jnp.int32)
    for power in range(factors_in.shape[1] - 1):
        levels = levels + (crossed >= 1 << power).astype(jnp.int32)
    causal = row_pos >= col_pos
    weights = jnp.zeros((factors_in.shape[0], rows_count, rows_count), jnp.float32)
    for level in range(factors_in.shape[1]):
        weights = weights + jnp.where((levels == level)[None], factors_in[:, level, :, None], jnp.float32(0.0))
    return jnp.where(causal[None], weights, jnp.float32(0.0))

def block_rows(rows, block):
    piece = rows[block * TOK_DEV:(block + 1) * TOK_DEV]
    return jnp.transpose(piece.reshape(TOK_DEV, H, DH), (1, 0, 2)).astype(jnp.float32)

def to_half(values):
    return lax.optimization_barrier(values.astype(jnp.bfloat16)).astype(jnp.float32)

def attend(queries, key_rows, value_rows, weights, factors_x, buckets, scale):
    scores = jnp.einsum('htd,hsd->hts', queries, key_rows)
    probs_wide = to_half(scale * scores * weights)
    inner = jnp.einsum('hts,hsd->htd', probs_wide, value_rows)
    reads = jnp.einsum('htd,lhde->lhte', queries, buckets)
    outer = lax.optimization_barrier(jnp.sum(jnp.transpose(factors_x, (1, 0, 2))[..., None] * reads, axis=0))
    return ((inner + scale * outer).astype(jnp.bfloat16), probs_wide)

def reference(inputs, level_factors, out_grad, master, moment_one, moment_two):
    blocks = TOKENS // TOK_DEV
    depth = blocks.bit_length() - 1
    scale = 1.0 / math.sqrt(DH * TOK_DEV)
    weights_b = master.astype(jnp.bfloat16)
    projected = [jnp.dot(inputs, weights_b[index], preferred_element_type=jnp.float32).astype(jnp.bfloat16) for index in range(3)]
    states = []
    for block in range(blocks):
        states.append(jnp.einsum('htd,hte->hde', block_rows(projected[1], block), block_rows(projected[2], block)))
    zero_state = jnp.zeros((H, DH, DH), jnp.float32)

    def bucket_of(block):
        levels = []
        for level in range(LV_OUT):
            if level < depth and block >> level & 1 == 1:
                base = block >> level + 1 << level + 1
                total = zero_state
                for other in range(base, base + (1 << level)):
                    total = total + states[other]
                levels.append(total)
            else:
                levels.append(zero_state)
        return to_half(jnp.stack(levels))
    outputs = []
    dstates = []
    for block in range(blocks):
        queries = block_rows(projected[0], block)
        span = slice(block * TOK_DEV, (block + 1) * TOK_DEV)
        factors_x = level_factors[:, LV_IN:, span]
        weights = inner_weights(level_factors[:, :LV_IN, span])
        result, probs = attend(queries, block_rows(projected[1], block), block_rows(projected[2], block), weights, factors_x, bucket_of(block), scale)
        outputs.append(jnp.transpose(result, (1, 0, 2)).reshape(TOK_DEV, H * DH))
        grad_rows = block_rows(out_grad, block)
        weighted = to_half(factors_x[:, :, :, None] * grad_rows[:, None])
        dstates.append(scale * jnp.einsum('htd,hlte->lhde', queries, weighted))
    attention = jnp.concatenate(outputs, axis=0)
    grads_rows = [[], [], []]
    for block in range(blocks):
        incoming = zero_state
        for level in range(depth):
            if block >> level & 1 == 0:
                base = block >> level + 1 << level + 1
                for other in range(base + (1 << level), base + (2 << level)):
                    incoming = incoming + dstates[other][level]
        incoming = to_half(incoming)
        queries = block_rows(projected[0], block)
        key_rows = block_rows(projected[1], block)
        value_rows = block_rows(projected[2], block)
        span = slice(block * TOK_DEV, (block + 1) * TOK_DEV)
        factors_x = level_factors[:, LV_IN:, span]
        weights = inner_weights(level_factors[:, :LV_IN, span])
        buckets = bucket_of(block)
        result, probs = attend(queries, key_rows, value_rows, weights, factors_x, buckets, scale)
        grad_rows = block_rows(out_grad, block)
        grad_probs = jnp.einsum('htd,hsd->hts', grad_rows, value_rows)
        mixed = to_half(scale * grad_probs * weights)
        backs = jnp.einsum('hte,lhde->lhtd', grad_rows, buckets)
        outer_q = lax.optimization_barrier(jnp.sum(jnp.transpose(factors_x, (1, 0, 2))[..., None] * backs, axis=0))
        grad_q = jnp.einsum('hts,hsd->htd', mixed, key_rows) + scale * outer_q
        grad_k = jnp.einsum('hts,htd->hsd', mixed, queries) + jnp.einsum('hse,hde->hsd', value_rows, incoming)
        grad_v = jnp.einsum('hts,htd->hsd', probs, grad_rows) + jnp.einsum('hsd,hde->hse', key_rows, incoming)
        for index, grad_block in enumerate((grad_q, grad_k, grad_v)):
            grads_rows[index].append(jnp.transpose(grad_block, (1, 0, 2)).reshape(TOK_DEV, H * DH).astype(jnp.bfloat16))
    fresh = []
    for index in range(3):
        grad_all = jnp.concatenate(grads_rows[index], axis=0)
        grad = jnp.dot(inputs.T, grad_all, preferred_element_type=jnp.float32) / TOKENS
        first = 0.9 * moment_one[index] + 0.1 * grad
        second = 0.95 * moment_two[index] + 0.05 * grad * grad
        updated = master[index] - 0.003 * (first / (jnp.sqrt(second) + 1e-08) + 0.1 * master[index])
        fresh.append(updated.astype(jnp.bfloat16))
    return (attention, jnp.stack(fresh))
```

```python
import functools
import math

import jax
import jax.numpy as jnp
from jax import lax
from jax.experimental import pallas as pl
from jax.experimental.pallas import tpu as pltpu
from jax.sharding import PartitionSpec as P

LV_IN = 8
MESH = pl.DeviceIdType.MESH
F32 = jnp.float32
BF16 = jnp.bfloat16
VMEM_LIMIT = 56 * 1024 * 1024


def factor_ctx(count):
    nx = 1 << ((count.bit_length() - 1) // 2)
    return count // nx, nx


class Gather:
    def __init__(self, ref, nz, nx, rows, sz, rz, sx, rx):
        self.ref, self.nz, self.nx, self.rows = ref, nz, nx, rows
        self.sz, self.rz, self.sx, self.rx = sz, rz, sx, rx
        me = lax.axis_index("ctx")
        self.z, self.x = me // nx, me % nx
        self.started = []

    def piece(self, i, d, z, x):
        half = self.rows // 2
        start = pl.multiple_of((z * self.nx + x) * self.rows + d * half, half)
        return self.ref.at[i, pl.ds(start, half), :]

    def origin(self, d, t):
        return (self.z + (self.nz - t if d == 0 else t)) % self.nz

    def ring_peer(self, d):
        return ((self.z + (1 if d == 0 else self.nz - 1)) % self.nz) * self.nx + self.x

    def ring_copy(self, i, d, s, z):
        view = self.piece(i, d, z, self.x)
        return pltpu.make_async_remote_copy(
            src_ref=view, dst_ref=view, send_sem=self.sz.at[i, d, s], recv_sem=self.rz.at[i, d, s],
            device_id={"ctx": self.ring_peer(d)}, device_id_type=MESH)

    def side_copy(self, i, d, t, p, x):
        view = self.piece(i, d, self.origin(d, t), x)
        return pltpu.make_async_remote_copy(
            src_ref=view, dst_ref=view, send_sem=self.sx.at[i, d, t, p - 1], recv_sem=self.rx.at[i, d, t, p - 1],
            device_id={"ctx": self.z * self.nx + (self.x + p) % self.nx}, device_id_type=MESH)

    def send(self, i, d, t):
        if t < self.nz - 1:
            copy = self.ring_copy(i, d, t, self.origin(d, t))
            copy.start()
            self.started.append(copy)
        for p in range(1, self.nx):
            copy = self.side_copy(i, d, t, p, self.x)
            copy.start()
            self.started.append(copy)

    def ring_step(self, i, d, s):
        self.ring_copy(i, d, s, self.origin(d, s + 1)).wait_recv()
        self.send(i, d, s + 1)

    def wait_side(self, i):
        for t in range(self.nz):
            for d in range(2):
                for p in range(1, self.nx):
                    self.side_copy(i, d, t, p, (self.x + self.nx - p) % self.nx).wait_recv()

    def finish(self):
        for copy in self.started:
            copy.wait_send()


def ctx_peers(nz, nx):
    me = lax.axis_index("ctx")
    z, x = me // nx, me % nx
    peers = [{"ctx": ((z + 1) % nz) * nx + x}, {"ctx": ((z + nz - 1) % nz) * nx + x}]
    peers += [{"ctx": z * nx + (x + p) % nx} for p in range(1, nx)]
    return peers


def greet(peers):
    barrier = pltpu.get_barrier_semaphore()
    for peer in peers:
        pl.semaphore_signal(barrier, inc=1, device_id=peer, device_id_type=MESH)
    pl.semaphore_wait(barrier, len(peers))


def project_kernel(nz, nx, nh, x_ref, m_ref, p_ref, xt_ref, xs, ws, sz, rz, sx, rx, sy, ry, sc, rc):
    rows = m_ref.shape[1]
    width = x_ref.shape[1]
    ny = nh // 2
    head = lax.axis_index("head")
    y, core = head // 2, head % 2
    sibling = {"head": y * 2 + 1 - core}
    peers = ctx_peers(nz, nx) + [sibling]
    peers += [{"head": ((y + p) % ny) * 2 + core} for p in range(1, ny)]
    gather = Gather(ws, nz, nx, rows, sz, rz, sx, rx)
    own = pl.multiple_of(lax.axis_index("ctx") * rows, rows)
    for i in range(3):
        ws[i, pl.ds(own, rows), :] = m_ref[i].astype(BF16)

    def columns(h):
        return xs.at[:, pl.ds(pl.multiple_of(h * width, width), width)]

    greet(peers)
    xs[:, pl.ds(pl.multiple_of(head * width, width), width)] = x_ref[...]
    started = []

    def y_copy(p, h):
        return pltpu.make_async_remote_copy(
            src_ref=columns(h), dst_ref=columns(h), send_sem=sy.at[p], recv_sem=ry.at[p],
            device_id={"head": ((y + p) % ny) * 2 + core}, device_id_type=MESH)

    def core_copy(p, h):
        return pltpu.make_async_remote_copy(
            src_ref=columns(h), dst_ref=columns(h), send_sem=sc.at[p], recv_sem=rc.at[p],
            device_id=sibling, device_id_type=MESH)

    for i in range(3):
        for d in range(2):
            gather.send(i, d, 0)
        if i == 0:
            for p in range(1, ny):
                started.append(y_copy(p, head))
                started[-1].start()
            started.append(core_copy(0, head))
            started[-1].start()

    def ring(i):
        for s in range(nz - 1):
            for d in range(2):
                gather.ring_step(i, d, s)

    def dots(i):
        tile = min(512, xs.shape[0])

        @pl.loop(0, xs.shape[0] // tile)
        def _(r):
            span = pl.ds(pl.multiple_of(r * tile, tile), tile)
            p_ref[i, span, :] = jnp.dot(xs[span, :], ws[i], preferred_element_type=F32).astype(BF16)

    ring(0)
    for p in range(1, ny):
        source = ((y + ny - p) % ny) * 2 + core
        y_copy(p, source).wait_recv()
        started.append(core_copy(p, source))
        started[-1].start()
    ring(1)
    for p in range(ny):
        core_copy(p, ((y + ny - p) % ny) * 2 + 1 - core).wait_recv()
    piece = min(256, width)

    @pl.loop(0, xs.shape[1] // piece)
    def _(r):
        span = pl.ds(pl.multiple_of(r * piece, piece), piece)
        xt_ref[span, :] = xs[:, span].T

    ring(2)
    for i in range(3):
        gather.wait_side(i)
        dots(i)
    gather.finish()
    for copy in started:
        copy.wait_send()


def project(inputs, master, nz, nx, nh):
    tokens, width = inputs.shape
    rows, cols = master.shape[1:]
    features = width * nh
    dma = pltpu.SemaphoreType.DMA
    ny = nh // 2
    vmem = pl.BlockSpec(memory_space=pltpu.VMEM)
    return pl.pallas_call(
        functools.partial(project_kernel, nz, nx, nh),
        out_shape=(jax.ShapeDtypeStruct((3, tokens, cols), BF16), jax.ShapeDtypeStruct((features, tokens), BF16)),
        in_specs=[vmem] * 2,
        out_specs=(vmem, vmem),
        scratch_shapes=[
            pltpu.VMEM((tokens, features), BF16),
            pltpu.VMEM((3, features, cols), BF16),
            dma((3, 2, nz - 1)), dma((3, 2, nz - 1)),
            dma((3, 2, nz, nx - 1)), dma((3, 2, nz, nx - 1)),
            dma((ny,)), dma((ny,)), dma((ny,)), dma((ny,)),
        ],
        compiler_params=pltpu.CompilerParams(collective_id=0, has_side_effects=True, vmem_limit_bytes=VMEM_LIMIT),
    )(inputs, master)


def update_kernel(nz, nx, xt_ref, g_ref, m_ref, m1_ref, m2_ref, out_ref,
                  own, xsend, xrecv, zsend, zrecv, ssx, rsx, ssz, rsz, sz, rz, sx, rx):
    rows = m_ref.shape[1]
    half = rows // 2
    tokens = g_ref.shape[1] * lax.axis_size("ctx")
    me = lax.axis_index("ctx")
    z, x = me // nx, me % nx
    gather = Gather(out_ref, nz, nx, rows, sz, rz, sx, rx)
    greet(ctx_peers(nz, nx))
    started = []

    def product(i, zb, xb):
        start = pl.multiple_of((zb * nx + xb) * rows, rows)
        return jnp.dot(xt_ref[pl.ds(start, rows), :], g_ref[i], preferred_element_type=F32)

    def x_copy(i, delta, p):
        return pltpu.make_async_remote_copy(
            src_ref=xsend.at[i, delta, p - 1], dst_ref=xrecv.at[i, delta, p - 1],
            send_sem=ssx.at[i, delta, p - 1], recv_sem=rsx.at[i, delta, p - 1],
            device_id={"ctx": z * nx + (x + p) % nx}, device_id_type=MESH)

    def z_copy(i, d, t):
        return pltpu.make_async_remote_copy(
            src_ref=zsend.at[i, d, t], dst_ref=zrecv.at[i, d, t],
            send_sem=ssz.at[i, d, t], recv_sem=rsz.at[i, d, t],
            device_id={"ctx": gather.ring_peer(d)}, device_id_type=MESH)

    order = []
    for k in range(1, nz // 2 + 1):
        order += [k] if k == nz - k else [k, nz - k]
    order.append(0)

    def partials(i):
        for delta in order:
            for p in range(1, nx):
                xsend[i, delta, p - 1] = product(i, (z + delta) % nz, (x + p) % nx).astype(BF16)
                started.append(x_copy(i, delta, p))
                started[-1].start()
        for delta in order:
            own[i, delta] = product(i, (z + delta) % nz, x)

    arrived = set()

    def reduce_step(i, d, t):
        delta = (nz - 1 - t) if d == 0 else (t + 1) % nz
        for p in range(1, nx):
            if (i, delta, p) not in arrived:
                arrived.add((i, delta, p))
                x_copy(i, delta, p).wait_recv()
        part = slice(d * half, (d + 1) * half)
        total = own[i, delta, part, :]
        for p in range(1, nx):
            total = total + xrecv[i, delta, p - 1, part, :].astype(F32)
        if t > 0:
            z_copy(i, d, t - 1).wait_recv()
            total = total + zrecv[i, d, t - 1].astype(F32)
        if t < nz - 1:
            zsend[i, d, t] = total.astype(BF16)
            started.append(z_copy(i, d, t))
            started[-1].start()
            return
        grad = total / tokens
        master = m_ref[i, part, :]
        first = 0.9 * m1_ref[i, part, :] + 0.1 * grad
        second = 0.95 * m2_ref[i, part, :] + 0.05 * grad * grad
        updated = master - 0.003 * (first / (jnp.sqrt(second) + 1e-08) + 0.1 * master)
        start = pl.multiple_of(me * rows + d * half, half)
        out_ref[i, pl.ds(start, half), :] = updated.astype(BF16)
        gather.send(i, d, 0)

    for i in range(3):
        partials(i)
    for i in range(4):
        for t in range(nz):
            for d in range(2):
                if i < 3:
                    reduce_step(i, d, t)
                if i > 0 and t < nz - 1:
                    gather.ring_step(i - 1, d, t)
    for i in range(3):
        gather.wait_side(i)
    gather.finish()
    for copy in started:
        copy.wait_send()


def update(xt, grads, master, moment_one, moment_two, nz, nx):
    rows, cols = master.shape[1:]
    dma = pltpu.SemaphoreType.DMA
    vmem = pl.BlockSpec(memory_space=pltpu.VMEM)
    return pl.pallas_call(
        functools.partial(update_kernel, nz, nx),
        out_shape=jax.ShapeDtypeStruct((3, xt.shape[0], cols), BF16),
        in_specs=[vmem] * 5,
        out_specs=vmem,
        scratch_shapes=[
            pltpu.VMEM((3, nz, rows, cols), F32),
            pltpu.VMEM((3, nz, nx - 1, rows, cols), BF16),
            pltpu.VMEM((3, nz, nx - 1, rows, cols), BF16),
            pltpu.VMEM((3, 2, nz - 1, rows // 2, cols), BF16),
            pltpu.VMEM((3, 2, nz - 1, rows // 2, cols), BF16),
            dma((3, nz, nx - 1)), dma((3, nz, nx - 1)),
            dma((3, 2, nz - 1)), dma((3, 2, nz - 1)),
            dma((3, 2, nz - 1)), dma((3, 2, nz - 1)),
            dma((3, 2, nz, nx - 1)), dma((3, 2, nz, nx - 1)),
        ],
        compiler_params=pltpu.CompilerParams(collective_id=1, has_side_effects=True, vmem_limit_bytes=VMEM_LIMIT),
    )(xt, grads, master, moment_one, moment_two)


def dot_t(a, b):
    return lax.dot_general(a, b, (((0,), (0,)), ((), ())), preferred_element_type=F32)


def dot_nt(a, b):
    return lax.dot_general(a, b, (((1,), (1,)), ((), ())), preferred_element_type=F32)


def states_kernel(scale, depth, p_ref, g_ref, f_ref, own_ref, pend_ref):
    queries = p_ref[0]
    own_ref[0] = dot_t(p_ref[1], p_ref[2])
    grads = g_ref[...].astype(F32)
    for level in range(depth):
        weighted = (f_ref[0, :, LV_IN + level:LV_IN + level + 1] * grads).astype(BF16)
        pend_ref[level, 0] = scale * dot_t(queries, weighted)


def inner_kernel(scale, tile, p_ref, g_ref, f_ref, att_ref, dq_ref, dk_ref, dv_ref):
    tokens = g_ref.shape[0]
    top = f_ref[0, :, LV_IN - 1:LV_IN]
    row = lax.broadcasted_iota(jnp.int32, (tile, tile), 0)
    col = lax.broadcasted_iota(jnp.int32, (tile, tile), 1)
    crossed = jnp.bitwise_xor(row, col)
    causal = row >= col
    for b in range(tokens // tile):
        span = slice(b * tile, (b + 1) * tile)
        queries, grads = p_ref[0, span, :], g_ref[span, :]
        weights = jnp.broadcast_to(f_ref[0, span, 0:1], (tile, tile))
        for level in range(1, LV_IN):
            factor = f_ref[0, span, level:level + 1]
            weights = jnp.where(crossed >= 1 << (level - 1), factor, weights)
        weights = jnp.where(causal, weights, 0.0)
        rest = top[span]
        if b:
            weights = jnp.concatenate([jnp.broadcast_to(rest, (tile, b * tile)), weights], axis=1)
        seen = slice(0, (b + 1) * tile)
        keys, values = p_ref[1, seen, :], p_ref[2, seen, :]
        probs = (scale * dot_nt(queries, keys) * weights).astype(BF16)
        mixed = (scale * dot_nt(grads, values) * weights).astype(BF16)
        att_ref[span, :] = jnp.dot(probs, values, preferred_element_type=F32)
        dq_ref[span, :] = jnp.dot(mixed, keys, preferred_element_type=F32)
        to_keys = dot_t(mixed, queries)
        to_values = dot_t(probs, grads)
        if b:
            before = slice(0, b * tile)
            dk_ref[before, :] += to_keys[before]
            dv_ref[before, :] += to_values[before]
        dk_ref[span, :] = to_keys[b * tile:]
        dv_ref[span, :] = to_values[b * tile:]


def outer_kernel(scale, depth, p_ref, g_ref, f_ref, b_ref, i_ref, att_ref, dq_ref, dk_ref, dv_ref, out_ref, grad_ref):
    queries, grads = p_ref[0], g_ref[...]
    outer = jnp.zeros(att_ref.shape, F32)
    back = jnp.zeros(att_ref.shape, F32)
    for level in range(depth):
        factor = f_ref[0, :, LV_IN + level:LV_IN + level + 1]
        outer = outer + factor * jnp.dot(queries, b_ref[level, 0], preferred_element_type=F32)
        back = back + factor * dot_nt(grads, b_ref[level, 0])
    out_ref[...] = (att_ref[...] + scale * outer).astype(BF16)
    grad_ref[0] = (dq_ref[...] + scale * back).astype(BF16)
    grad_ref[1] = (dk_ref[...] + dot_nt(p_ref[2], i_ref[0])).astype(BF16)
    grad_ref[2] = (dv_ref[...] + jnp.dot(p_ref[1], i_ref[0], preferred_element_type=F32)).astype(BF16)


def from_partner(value, axis, apart):
    mask = 2**apart
    pairs = [(source, source ^ mask) for source in range(lax.axis_size(axis))]
    return lax.ppermute(value, axis, pairs)


def body(inputs, level_factors, out_grad, master, moment_one, moment_two):
    tokens_dev = inputs.shape[0]
    heads = level_factors.shape[0]
    head_size = out_grad.shape[1] // heads
    levels = level_factors.shape[1]
    block_index = lax.axis_index("ctx")
    blocks = lax.axis_size("ctx")
    nz, nx = factor_ctx(blocks)
    depth = min(blocks.bit_length() - 1, levels - LV_IN)
    scale = 1.0 / math.sqrt(head_size * tokens_dev)
    factors = jnp.transpose(level_factors, (0, 2, 1))
    projected, xt = project(inputs, master, nz, nx, lax.axis_size("head"))

    p_spec = pl.BlockSpec((3, tokens_dev, head_size), lambda h: (0, 0, h))
    g_spec = pl.BlockSpec((tokens_dev, head_size), lambda h: (0, h))
    f_spec = pl.BlockSpec((1, tokens_dev, levels), lambda h: (h, 0, 0))
    s_spec = pl.BlockSpec((1, head_size, head_size), lambda h: (h, 0, 0))
    l_spec = pl.BlockSpec((depth, 1, head_size, head_size), lambda h: (0, h, 0, 0))
    params = pltpu.CompilerParams(vmem_limit_bytes=VMEM_LIMIT)
    wide = jax.ShapeDtypeStruct((tokens_dev, heads * head_size), F32)
    narrow = jax.ShapeDtypeStruct((tokens_dev, heads * head_size), BF16)
    own_state, pending = pl.pallas_call(
        functools.partial(states_kernel, scale, depth),
        grid=(heads,),
        out_shape=(jax.ShapeDtypeStruct((heads, head_size, head_size), F32),
                   jax.ShapeDtypeStruct((depth, heads, head_size, head_size), F32)),
        in_specs=[p_spec, g_spec, f_spec],
        out_specs=(s_spec, l_spec),
        compiler_params=params,
    )(projected, out_grad, factors)

    square = tokens_dev * tokens_dev * head_size * heads
    inner, dq, dk, dv = pl.pallas_call(
        functools.partial(inner_kernel, scale, min(256, tokens_dev)),
        grid=(heads,),
        out_shape=(wide,) * 4,
        in_specs=[p_spec, g_spec, f_spec],
        out_specs=(g_spec,) * 4,
        compiler_params=params,
        cost_estimate=pl.CostEstimate(flops=12 * square, bytes_accessed=24 * tokens_dev * heads * head_size, transcendentals=0),
    )(projected, out_grad, factors)

    running = own_state
    buckets = []
    for level in range(depth):
        other = from_partner(running, "ctx", level)
        upper = (block_index >> level & 1) == 1
        buckets.append(jnp.where(upper, other, 0.0).astype(BF16))
        running = running + other
    buckets_b = jnp.stack(buckets)
    incoming = jnp.zeros((heads, head_size, head_size), F32)
    for level in range(depth):
        partner = from_partner(pending[level:depth].astype(BF16), "ctx", level).astype(F32)
        lower = (block_index >> level & 1) == 0
        incoming = incoming + jnp.where(lower, partner[0], 0.0)
        if level + 1 < depth:
            pending = pending.at[level + 1:depth].add(partner[1:])
    incoming_b = incoming.astype(BF16)

    attention, grads = pl.pallas_call(
        functools.partial(outer_kernel, scale, depth),
        grid=(heads,),
        out_shape=(narrow, jax.ShapeDtypeStruct((3, tokens_dev, heads * head_size), BF16)),
        in_specs=[p_spec, g_spec, f_spec, l_spec, s_spec] + [g_spec] * 4,
        out_specs=(g_spec, p_spec),
        compiler_params=params,
    )(projected, out_grad, factors, buckets_b, incoming_b, inner, dq, dk, dv)

    new_weights = update(xt, grads, master, moment_one, moment_two, nz, nx)
    return (attention, new_weights)


def solution(mesh):
    placed = (
        P("ctx", "head"),
        P("head", None, "ctx"),
        P("ctx", "head"),
        P(None, "ctx", "head"),
        P(None, "ctx", "head"),
        P(None, "ctx", "head"),
    )
    return jax.shard_map(
        body,
        mesh=mesh,
        in_specs=placed,
        out_specs=(P("ctx", "head"), P(None, None, "head")),
        check_vma=False,
    )
```

```python
import functools
import math

import jax
import jax.numpy as jnp
from jax import lax
from jax.experimental import pallas as pl
from jax.experimental.pallas import tpu as pltpu
from jax.sharding import PartitionSpec as P

LV_IN = 8
MESH = pl.DeviceIdType.MESH
WIDE = ((1, 1),)
F32 = jnp.float32
BF16 = jnp.bfloat16
VMEM_LIMIT = 60 * 1024 * 1024


def factor_ctx(count):
    nx = 1 << ((count.bit_length() - 1) // 2)
    return count // nx, nx


class Gather:
    def __init__(self, ref, nz, nx, rows, sz, rz, sx, rx):
        self.ref, self.nz, self.nx, self.rows = ref, nz, nx, rows
        self.sz, self.rz, self.sx, self.rx = sz, rz, sx, rx
        me = lax.axis_index("ctx")
        self.z, self.x = me // nx, me % nx
        self.started = []

    def piece(self, i, d, z, x):
        half = self.rows // 2
        start = pl.multiple_of((z * self.nx + x) * self.rows + d * half, half)
        return self.ref.at[i, pl.ds(start, half), :]

    def origin(self, d, t):
        return (self.z + (self.nz - t if d == 0 else t)) % self.nz

    def ring_peer(self, d):
        return ((self.z + (1 if d == 0 else self.nz - 1)) % self.nz) * self.nx + self.x

    def ring_copy(self, i, d, s, z, q):
        view = self.piece(i, d, z, (self.x + q) % self.nx)
        return pltpu.make_async_remote_copy(
            src_ref=view, dst_ref=view, send_sem=self.sz.at[i, d, s, q], recv_sem=self.rz.at[i, d, s, q],
            device_id={"ctx": self.ring_peer(d)}, device_id_type=MESH)

    def side_copy(self, i, d, t, p, x):
        view = self.piece(i, d, self.origin(d, t), x)
        return pltpu.make_async_remote_copy(
            src_ref=view, dst_ref=view, send_sem=self.sx.at[i, d, t, p - 1], recv_sem=self.rx.at[i, d, t, p - 1],
            device_id={"ctx": self.z * self.nx + (self.x + p) % self.nx}, device_id_type=MESH)

    def start(self, copy):
        copy.start()
        self.started.append(copy)

    def send(self, i, d, t):
        if t < self.nz - 1:
            self.start(self.ring_copy(i, d, t, self.origin(d, t), 0))
        for p in range(1, self.nx):
            self.start(self.side_copy(i, d, t, p, self.x))

    def inject(self, i, d):
        for p in range(1, self.nx):
            self.side_copy(i, d, 0, p, (self.x + self.nx - p) % self.nx).wait_recv()
            self.start(self.ring_copy(i, d, 0, self.z, self.nx - p))

    def ring_step(self, i, d, s):
        wide = (i, d) in WIDE
        if wide and s == 0:
            self.inject(i, d)
        for q in range(self.nx if wide else 1):
            self.ring_copy(i, d, s, self.origin(d, s + 1), q).wait_recv()
            if wide and s + 1 < self.nz - 1:
                self.start(self.ring_copy(i, d, s + 1, self.origin(d, s + 1), q))
        if not wide:
            self.send(i, d, s + 1)

    def wait_side(self, i):
        for t in range(self.nz):
            for d in range(2):
                if (i, d) not in WIDE:
                    for p in range(1, self.nx):
                        self.side_copy(i, d, t, p, (self.x + self.nx - p) % self.nx).wait_recv()

    def finish(self):
        for copy in self.started:
            copy.wait_send()


def ctx_peers(nz, nx):
    me = lax.axis_index("ctx")
    z, x = me // nx, me % nx
    peers = [{"ctx": ((z + 1) % nz) * nx + x}, {"ctx": ((z + nz - 1) % nz) * nx + x}]
    peers += [{"ctx": z * nx + (x + p) % nx} for p in range(1, nx)]
    return peers


def greet(peers):
    barrier = pltpu.get_barrier_semaphore()
    for peer in peers:
        pl.semaphore_signal(barrier, inc=1, device_id=peer, device_id_type=MESH)
    pl.semaphore_wait(barrier, len(peers))


def project_kernel(nz, nx, nh, x_ref, m_ref, f_ref, p_ref, xt_ref, ft_ref, xs, ws, sz, rz, sx, rx, sy, ry, sc, rc):
    rows = m_ref.shape[1]
    width = x_ref.shape[1]
    ny = nh // 2
    head = lax.axis_index("head")
    y, core = head // 2, head % 2
    sibling = {"head": y * 2 + 1 - core}
    peers = ctx_peers(nz, nx) + [sibling]
    peers += [{"head": ((y + p) % ny) * 2 + core} for p in range(1, ny)]
    gather = Gather(ws, nz, nx, rows, sz, rz, sx, rx)
    own = pl.multiple_of(lax.axis_index("ctx") * rows, rows)
    for i in range(3):
        ws[i, pl.ds(own, rows), :] = m_ref[i].astype(BF16)

    def columns(h):
        return xs.at[:, pl.ds(pl.multiple_of(h * width, width), width)]

    greet(peers)
    xs[:, pl.ds(pl.multiple_of(head * width, width), width)] = x_ref[...]
    started = []

    def y_copy(p, h):
        return pltpu.make_async_remote_copy(
            src_ref=columns(h), dst_ref=columns(h), send_sem=sy.at[p], recv_sem=ry.at[p],
            device_id={"head": ((y + p) % ny) * 2 + core}, device_id_type=MESH)

    def core_copy(p, h):
        return pltpu.make_async_remote_copy(
            src_ref=columns(h), dst_ref=columns(h), send_sem=sc.at[p], recv_sem=rc.at[p],
            device_id=sibling, device_id_type=MESH)

    for i in range(3):
        for d in range(2):
            gather.send(i, d, 0)
        if i == 0:
            for p in range(1, ny):
                started.append(y_copy(p, head))
                started[-1].start()
            started.append(core_copy(0, head))
            started[-1].start()

    def ring(i):
        for s in range(nz - 1):
            for d in range(2):
                gather.ring_step(i, d, s)

    def dots(i):
        tile = min(512, xs.shape[0])

        @pl.loop(0, xs.shape[0] // tile)
        def _(r):
            span = pl.ds(pl.multiple_of(r * tile, tile), tile)
            p_ref[i, span, :] = jnp.dot(xs[span, :], ws[i], preferred_element_type=F32).astype(BF16)

    for h in range(f_ref.shape[0]):
        ft_ref[h] = f_ref[h].T
    ring(0)
    for p in range(1, ny):
        source = ((y + ny - p) % ny) * 2 + core
        y_copy(p, source).wait_recv()
        started.append(core_copy(p, source))
        started[-1].start()
    ring(1)
    for p in range(ny):
        core_copy(p, ((y + ny - p) % ny) * 2 + 1 - core).wait_recv()
    piece = min(256, width)

    @pl.loop(0, xs.shape[1] // piece)
    def _(r):
        span = pl.ds(pl.multiple_of(r * piece, piece), piece)
        xt_ref[span, :] = xs[:, span].T

    ring(2)
    for i in range(3):
        gather.wait_side(i)
        dots(i)
    gather.finish()
    for copy in started:
        copy.wait_send()


def project(inputs, master, factors, nz, nx, nh):
    tokens, width = inputs.shape
    rows, cols = master.shape[1:]
    features = width * nh
    dma = pltpu.SemaphoreType.DMA
    ny = nh // 2
    vmem = pl.BlockSpec(memory_space=pltpu.VMEM)
    return pl.pallas_call(
        functools.partial(project_kernel, nz, nx, nh),
        out_shape=(jax.ShapeDtypeStruct((3, tokens, cols), BF16), jax.ShapeDtypeStruct((features, tokens), BF16),
                   jax.ShapeDtypeStruct((factors.shape[0], tokens, factors.shape[1]), F32)),
        in_specs=[vmem] * 3,
        out_specs=(vmem,) * 3,
        scratch_shapes=[
            pltpu.VMEM((tokens, features), BF16),
            pltpu.VMEM((3, features, cols), BF16),
            dma((3, 2, nz - 1, nx)), dma((3, 2, nz - 1, nx)),
            dma((3, 2, nz, nx - 1)), dma((3, 2, nz, nx - 1)),
            dma((ny,)), dma((ny,)), dma((ny,)), dma((ny,)),
        ],
        compiler_params=pltpu.CompilerParams(collective_id=0, has_side_effects=True, vmem_limit_bytes=VMEM_LIMIT),
    )(inputs, master, factors)


def dot_t(a, b):
    return lax.dot_general(a, b, (((0,), (0,)), ((), ())), preferred_element_type=F32)


def dot_nt(a, b):
    return lax.dot_general(a, b, (((1,), (1,)), ((), ())), preferred_element_type=F32)


def inner_head(scale, tile, size, h, p_ref, g_ref, f_ref, acc):
    tokens = g_ref.shape[0]
    lane = pl.ds(pl.multiple_of(h * size, size), size)
    row = lax.broadcasted_iota(jnp.int32, (tile, tile), 0)
    col = lax.broadcasted_iota(jnp.int32, (tile, tile), 1)
    crossed = jnp.bitwise_xor(row, col)
    causal = row >= col
    for b in range(tokens // tile):
        span = slice(b * tile, (b + 1) * tile)
        queries, grads = p_ref[0, span, lane], g_ref[span, lane]
        weights = jnp.broadcast_to(f_ref[h, span, 0:1], (tile, tile))
        for level in range(1, LV_IN):
            factor = f_ref[h, span, level:level + 1]
            weights = jnp.where(crossed >= 1 << (level - 1), factor, weights)
        weights = jnp.where(causal, weights, 0.0)
        if b:
            rest = f_ref[h, span, LV_IN - 1:LV_IN]
            weights = jnp.concatenate([jnp.broadcast_to(rest, (tile, b * tile)), weights], axis=1)
        seen = slice(0, (b + 1) * tile)
        keys, values = p_ref[1, seen, lane], p_ref[2, seen, lane]
        probs = (scale * dot_nt(queries, keys) * weights).astype(BF16)
        mixed = (scale * dot_nt(grads, values) * weights).astype(BF16)
        acc[0, span, lane] = jnp.dot(probs, values, preferred_element_type=F32)
        acc[1, span, lane] = jnp.dot(mixed, keys, preferred_element_type=F32)
        to_keys = dot_t(mixed, queries)
        to_values = dot_t(probs, grads)
        if b:
            before = slice(0, b * tile)
            acc[2, before, lane] += to_keys[before]
            acc[3, before, lane] += to_values[before]
        acc[2, span, lane] = to_keys[b * tile:]
        acc[3, span, lane] = to_values[b * tile:]


def update_kernel(nz, nx, scale, depth, p_ref, g_ref, f_ref, xt_ref, m_ref, m1_ref, m2_ref, att_ref, out_ref,
                  acc, dy, sums, pend, sum_out, sum_in, pend_out, pend_in,
                  own, xsend, xrecv, zsend, zrecv, sse, rse, spe, rpe, ssx, rsx, ssz, rsz, sz, rz, sx, rx):
    rows = m_ref.shape[1]
    half = rows // 2
    heads = f_ref.shape[0]
    size = g_ref.shape[1] // heads
    tokens = g_ref.shape[0] * lax.axis_size("ctx")
    me = lax.axis_index("ctx")
    z, x = me // nx, me % nx
    gather = Gather(out_ref, nz, nx, rows, sz, rz, sx, rx)

    def partner(level):
        mask = 1 << level
        return {"ctx": me + mask - 2 * mask * (me // mask % 2)}

    greet(ctx_peers(nz, nx) + [partner(level) for level in range(depth)])
    started = []

    def exchange(level):
        return [
            pltpu.make_async_remote_copy(
                src_ref=sum_out.at[level], dst_ref=sum_in.at[level], send_sem=sse.at[level], recv_sem=rse.at[level],
                device_id=partner(level), device_id_type=MESH),
            pltpu.make_async_remote_copy(
                src_ref=pend_out.at[level, pl.ds(level, depth - level)],
                dst_ref=pend_in.at[level, pl.ds(level, depth - level)],
                send_sem=spe.at[level], recv_sem=rpe.at[level],
                device_id=partner(level), device_id_type=MESH)]

    def exchange_start(level):
        sum_out[level] = sums[...]
        pend_out[level, level:] = pend[level:].astype(BF16)
        for copy in exchange(level):
            copy.start()

    def exchange_end(level):
        for copy in exchange(level):
            copy.wait_recv()
        if level + 1 < depth:
            sums[...] += sum_in[level]
            pend[level + 1:] += pend_in[level, level + 1:].astype(F32)
            exchange_start(level + 1)

    @pl.loop(0, heads)
    def _(h):
        lane = pl.ds(pl.multiple_of(h * size, size), size)
        queries = p_ref[0, :, lane]
        sums[h] = dot_t(p_ref[1, :, lane], p_ref[2, :, lane])
        grads = g_ref[:, lane].astype(F32)
        for level in range(depth):
            weighted = (f_ref[h, :, LV_IN + level:LV_IN + level + 1] * grads).astype(BF16)
            pend[level, h] = scale * dot_t(queries, weighted)

    exchange_start(0)

    @pl.loop(0, heads)
    def _(h):
        inner_head(scale, min(256, g_ref.shape[0]), size, h, p_ref, g_ref, f_ref, acc)
        for level in range(depth):
            @pl.when(h == min(level, heads - 1))
            def _():
                exchange_end(level)

    @pl.loop(0, heads)
    def _(h):
        lane = pl.ds(pl.multiple_of(h * size, size), size)
        queries, grads = p_ref[0, :, lane], g_ref[:, lane]
        outer = jnp.zeros(queries.shape, F32)
        back = jnp.zeros(queries.shape, F32)
        for level in range(depth):
            factor = f_ref[h, :, LV_IN + level:LV_IN + level + 1]
            upper = jnp.full((size, size), (me >> level) & 1) == 1
            bucket = jnp.where(upper, sum_in[level, h], 0.0).astype(BF16)
            outer = outer + factor * jnp.dot(queries, bucket, preferred_element_type=F32)
            back = back + factor * dot_nt(grads, bucket)
        att_ref[:, lane] = (acc[0, :, lane] + scale * outer).astype(BF16)
        dy[0, :, lane] = (acc[1, :, lane] + scale * back).astype(BF16)

    def key_value_grads():
        @pl.loop(0, heads)
        def _(h):
            lane = pl.ds(pl.multiple_of(h * size, size), size)
            incoming = jnp.zeros((size, size), F32)
            for level in range(depth):
                lower = jnp.full((size, size), (me >> level) & 1) == 0
                incoming = incoming + jnp.where(lower, pend_in[level, level, h].astype(F32), 0.0)
            incoming = incoming.astype(BF16)
            dy[1, :, lane] = (acc[2, :, lane] + dot_nt(p_ref[2, :, lane], incoming)).astype(BF16)
            dy[2, :, lane] = (acc[3, :, lane] + jnp.dot(
                p_ref[1, :, lane], incoming, preferred_element_type=F32)).astype(BF16)

    def product(i, zb, xb):
        start = pl.multiple_of((zb * nx + xb) * rows, rows)
        return jnp.dot(xt_ref[pl.ds(start, rows), :], dy[i], preferred_element_type=F32)

    def x_copy(i, delta, p):
        return pltpu.make_async_remote_copy(
            src_ref=xsend.at[i, delta, p - 1], dst_ref=xrecv.at[i, delta, p - 1],
            send_sem=ssx.at[i, delta, p - 1], recv_sem=rsx.at[i, delta, p - 1],
            device_id={"ctx": z * nx + (x + p) % nx}, device_id_type=MESH)

    def z_copy(i, d, t):
        return pltpu.make_async_remote_copy(
            src_ref=zsend.at[i, d, t], dst_ref=zrecv.at[i, d, t],
            send_sem=ssz.at[i, d, t], recv_sem=rsz.at[i, d, t],
            device_id={"ctx": gather.ring_peer(d)}, device_id_type=MESH)

    order = []
    for k in range(1, nz // 2 + 1):
        order += [k] if k == nz - k else [k, nz - k]
    order.append(0)

    def side_partials(i):
        for delta in order:
            for p in range(1, nx):
                xsend[i, delta, p - 1] = product(i, (z + delta) % nz, (x + p) % nx).astype(BF16)
                started.append(x_copy(i, delta, p))
                started[-1].start()

    def own_partials(i):
        for delta in order:
            own[delta] = product(i, (z + delta) % nz, x)

    arrived = set()

    def reduce_step(i, d, t):
        delta = (nz - 1 - t) if d == 0 else (t + 1) % nz
        for p in range(1, nx):
            if (i, delta, p) not in arrived:
                arrived.add((i, delta, p))
                x_copy(i, delta, p).wait_recv()
        part = slice(d * half, (d + 1) * half)
        total = own[delta, part, :]
        for p in range(1, nx):
            total = total + xrecv[i, delta, p - 1, part, :].astype(F32)
        if t > 0:
            z_copy(i, d, t - 1).wait_recv()
            total = total + zrecv[i, d, t - 1].astype(F32)
        if t < nz - 1:
            zsend[i, d, t] = total.astype(BF16)
            started.append(z_copy(i, d, t))
            started[-1].start()
            return
        grad = total / tokens
        master = m_ref[i, part, :]
        first = 0.9 * m1_ref[i, part, :] + 0.1 * grad
        second = 0.95 * m2_ref[i, part, :] + 0.05 * grad * grad
        updated = master - 0.003 * (first / (jnp.sqrt(second) + 1e-08) + 0.1 * master)
        start = pl.multiple_of(me * rows + d * half, half)
        out_ref[i, pl.ds(start, half), :] = updated.astype(BF16)
        gather.send(i, d, 0)

    side_partials(0)
    key_value_grads()
    side_partials(1)
    side_partials(2)
    for i in range(4):
        if i < 3:
            own_partials(i)
        for t in range(nz):
            for d in range(2):
                if i < 3:
                    reduce_step(i, d, t)
                if i > 0 and t < nz - 1:
                    gather.ring_step(i - 1, d, t)
    for i in range(3):
        gather.wait_side(i)
    gather.finish()
    for level in range(depth):
        started += exchange(level)
    for copy in started:
        copy.wait_send()


def attend_and_update(projected, out_grad, factors, xt, master, moment_one, moment_two, nz, nx, scale, depth):
    rows, cols = master.shape[1:]
    heads, tokens = factors.shape[:2]
    size = cols // heads
    dma = pltpu.SemaphoreType.DMA
    vmem = pl.BlockSpec(memory_space=pltpu.VMEM)
    return pl.pallas_call(
        functools.partial(update_kernel, nz, nx, scale, depth),
        out_shape=(jax.ShapeDtypeStruct((tokens, cols), BF16), jax.ShapeDtypeStruct((3, xt.shape[0], cols), BF16)),
        in_specs=[vmem] * 7,
        out_specs=(vmem, vmem),
        scratch_shapes=[
            pltpu.VMEM((4, tokens, cols), F32),
            pltpu.VMEM((3, tokens, cols), BF16),
            pltpu.VMEM((heads, size, size), F32),
            pltpu.VMEM((depth, heads, size, size), F32),
            pltpu.VMEM((depth, heads, size, size), F32),
            pltpu.VMEM((depth, heads, size, size), F32),
            pltpu.VMEM((depth, depth, heads, size, size), BF16),
            pltpu.VMEM((depth, depth, heads, size, size), BF16),
            pltpu.VMEM((nz, rows, cols), F32),
            pltpu.VMEM((3, nz, nx - 1, rows, cols), BF16),
            pltpu.VMEM((3, nz, nx - 1, rows, cols), BF16),
            pltpu.VMEM((3, 2, nz - 1, rows // 2, cols), BF16),
            pltpu.VMEM((3, 2, nz - 1, rows // 2, cols), BF16),
            dma((depth,)), dma((depth,)), dma((depth,)), dma((depth,)),
            dma((3, nz, nx - 1)), dma((3, nz, nx - 1)),
            dma((3, 2, nz - 1)), dma((3, 2, nz - 1)),
            dma((3, 2, nz - 1, nx)), dma((3, 2, nz - 1, nx)),
            dma((3, 2, nz, nx - 1)), dma((3, 2, nz, nx - 1)),
        ],
        compiler_params=pltpu.CompilerParams(collective_id=1, has_side_effects=True, vmem_limit_bytes=VMEM_LIMIT),
    )(projected, out_grad, factors, xt, master, moment_one, moment_two)


def body(inputs, level_factors, out_grad, master, moment_one, moment_two):
    tokens_dev = inputs.shape[0]
    heads = level_factors.shape[0]
    head_size = out_grad.shape[1] // heads
    blocks = lax.axis_size("ctx")
    nz, nx = factor_ctx(blocks)
    depth = min(blocks.bit_length() - 1, level_factors.shape[1] - LV_IN)
    scale = 1.0 / math.sqrt(head_size * tokens_dev)
    projected, xt, factors = project(inputs, master, level_factors, nz, nx, lax.axis_size("head"))
    return attend_and_update(
        projected, out_grad, factors, xt, master, moment_one, moment_two, nz, nx, scale, depth)


def solution(mesh):
    placed = (
        P("ctx", "head"),
        P("head", None, "ctx"),
        P("ctx", "head"),
        P(None, "ctx", "head"),
        P(None, "ctx", "head"),
        P(None, "ctx", "head"),
    )
    return jax.shard_map(
        body,
        mesh=mesh,
        in_specs=placed,
        out_specs=(P("ctx", "head"), P(None, None, "head")),
        check_vma=False,
    )
```

```python
import functools
import math

import jax
import jax.numpy as jnp
from jax import lax
from jax.experimental import pallas as pl
from jax.experimental.pallas import tpu as pltpu
from jax.sharding import PartitionSpec as P

LV_IN = 8
MESH = pl.DeviceIdType.MESH
WIDE = ((1, 1),)
F32 = jnp.float32
BF16 = jnp.bfloat16
VMEM_LIMIT = 60 * 1024 * 1024


def factor_ctx(count):
    nx = 1 << ((count.bit_length() - 1) // 2)
    return count // nx, nx


class Gather:
    def __init__(self, ref, nz, nx, rows, sz, rz, sx, rx):
        self.ref, self.nz, self.nx, self.rows = ref, nz, nx, rows
        self.sz, self.rz, self.sx, self.rx = sz, rz, sx, rx
        me = lax.axis_index("ctx")
        self.z, self.x = me // nx, me % nx
        self.started = []

    def piece(self, i, d, z, x):
        half = self.rows // 2
        start = pl.multiple_of((z * self.nx + x) * self.rows + d * half, half)
        return self.ref.at[i, pl.ds(start, half), :]

    def origin(self, d, t):
        return (self.z + (self.nz - t if d == 0 else t)) % self.nz

    def ring_peer(self, d):
        return ((self.z + (1 if d == 0 else self.nz - 1)) % self.nz) * self.nx + self.x

    def ring_copy(self, i, d, s, z, q):
        view = self.piece(i, d, z, (self.x + q) % self.nx)
        return pltpu.make_async_remote_copy(
            src_ref=view, dst_ref=view, send_sem=self.sz.at[i, d, s, q], recv_sem=self.rz.at[i, d, s, q],
            device_id={"ctx": self.ring_peer(d)}, device_id_type=MESH)

    def side_copy(self, i, d, t, p, x):
        view = self.piece(i, d, self.origin(d, t), x)
        return pltpu.make_async_remote_copy(
            src_ref=view, dst_ref=view, send_sem=self.sx.at[i, d, t, p - 1], recv_sem=self.rx.at[i, d, t, p - 1],
            device_id={"ctx": self.z * self.nx + (self.x + p) % self.nx}, device_id_type=MESH)

    def start(self, copy):
        copy.start()
        self.started.append(copy)

    def send(self, i, d, t):
        if t < self.nz - 1:
            self.start(self.ring_copy(i, d, t, self.origin(d, t), 0))
        for p in range(1, self.nx):
            self.start(self.side_copy(i, d, t, p, self.x))

    def inject(self, i, d):
        for p in range(1, self.nx):
            self.side_copy(i, d, 0, p, (self.x + self.nx - p) % self.nx).wait_recv()
            self.start(self.ring_copy(i, d, 0, self.z, self.nx - p))

    def ring_step(self, i, d, s):
        wide = (i, d) in WIDE
        if wide and s == 0:
            self.inject(i, d)
        for q in range(self.nx if wide else 1):
            self.ring_copy(i, d, s, self.origin(d, s + 1), q).wait_recv()
            if wide and s + 1 < self.nz - 1:
                self.start(self.ring_copy(i, d, s + 1, self.origin(d, s + 1), q))
        if not wide:
            self.send(i, d, s + 1)

    def wait_side(self, i):
        for t in range(self.nz):
            for d in range(2):
                if (i, d) not in WIDE:
                    for p in range(1, self.nx):
                        self.side_copy(i, d, t, p, (self.x + self.nx - p) % self.nx).wait_recv()

    def finish(self):
        for copy in self.started:
            copy.wait_send()


def ctx_peers(nz, nx):
    me = lax.axis_index("ctx")
    z, x = me // nx, me % nx
    peers = [{"ctx": ((z + 1) % nz) * nx + x}, {"ctx": ((z + nz - 1) % nz) * nx + x}]
    peers += [{"ctx": z * nx + (x + p) % nx} for p in range(1, nx)]
    return peers


def greet(peers):
    barrier = pltpu.get_barrier_semaphore()
    for peer in peers:
        pl.semaphore_signal(barrier, inc=1, device_id=peer, device_id_type=MESH)
    pl.semaphore_wait(barrier, len(peers))


def project_kernel(nz, nx, nh, x_ref, m_ref, f_ref, p_ref, xt_ref, ft_ref, xs, ws, sz, rz, sx, rx, sy, ry, sc, rc):
    rows = m_ref.shape[1]
    width = x_ref.shape[1]
    ny = nh // 2
    head = lax.axis_index("head")
    y, core = head // 2, head % 2
    sibling = {"head": y * 2 + 1 - core}
    peers = ctx_peers(nz, nx) + [sibling]
    peers += [{"head": ((y + p) % ny) * 2 + core} for p in range(1, ny)]
    gather = Gather(ws, nz, nx, rows, sz, rz, sx, rx)
    own = pl.multiple_of(lax.axis_index("ctx") * rows, rows)
    for i in range(3):
        ws[i, pl.ds(own, rows), :] = m_ref[i].astype(BF16)

    def columns(h):
        return xs.at[:, pl.ds(pl.multiple_of(h * width, width), width)]

    greet(peers)
    xs[:, pl.ds(pl.multiple_of(head * width, width), width)] = x_ref[...]
    started = []

    def y_copy(p, h):
        return pltpu.make_async_remote_copy(
            src_ref=columns(h), dst_ref=columns(h), send_sem=sy.at[p], recv_sem=ry.at[p],
            device_id={"head": ((y + p) % ny) * 2 + core}, device_id_type=MESH)

    def core_copy(p, h):
        return pltpu.make_async_remote_copy(
            src_ref=columns(h), dst_ref=columns(h), send_sem=sc.at[p], recv_sem=rc.at[p],
            device_id=sibling, device_id_type=MESH)

    for i in range(3):
        for d in range(2):
            gather.send(i, d, 0)
        if i == 0:
            for p in range(1, ny):
                started.append(y_copy(p, head))
                started[-1].start()
            started.append(core_copy(0, head))
            started[-1].start()

    def ring(i):
        for s in range(nz - 1):
            for d in range(2):
                gather.ring_step(i, d, s)

    def dots(i):
        tile = min(512, xs.shape[0])

        @pl.loop(0, xs.shape[0] // tile)
        def _(r):
            span = pl.ds(pl.multiple_of(r * tile, tile), tile)
            p_ref[i, span, :] = jnp.dot(xs[span, :], ws[i], preferred_element_type=F32).astype(BF16)

    for h in range(f_ref.shape[0]):
        ft_ref[h] = f_ref[h].T
    ring(0)
    for p in range(1, ny):
        source = ((y + ny - p) % ny) * 2 + core
        y_copy(p, source).wait_recv()
        started.append(core_copy(p, source))
        started[-1].start()
    ring(1)
    for p in range(ny):
        core_copy(p, ((y + ny - p) % ny) * 2 + 1 - core).wait_recv()
    piece = min(256, width)

    @pl.loop(0, xs.shape[1] // piece)
    def _(r):
        span = pl.ds(pl.multiple_of(r * piece, piece), piece)
        xt_ref[span, :] = xs[:, span].T

    gather.wait_side(0)
    dots(0)
    ring(2)
    for i in range(1, 3):
        gather.wait_side(i)
        dots(i)
    gather.finish()
    for copy in started:
        copy.wait_send()


def project(inputs, master, factors, nz, nx, nh):
    tokens, width = inputs.shape
    rows, cols = master.shape[1:]
    features = width * nh
    dma = pltpu.SemaphoreType.DMA
    ny = nh // 2
    vmem = pl.BlockSpec(memory_space=pltpu.VMEM)
    return pl.pallas_call(
        functools.partial(project_kernel, nz, nx, nh),
        out_shape=(jax.ShapeDtypeStruct((3, tokens, cols), BF16), jax.ShapeDtypeStruct((features, tokens), BF16),
                   jax.ShapeDtypeStruct((factors.shape[0], tokens, factors.shape[1]), F32)),
        in_specs=[vmem] * 3,
        out_specs=(vmem,) * 3,
        scratch_shapes=[
            pltpu.VMEM((tokens, features), BF16),
            pltpu.VMEM((3, features, cols), BF16),
            dma((3, 2, nz - 1, nx)), dma((3, 2, nz - 1, nx)),
            dma((3, 2, nz, nx - 1)), dma((3, 2, nz, nx - 1)),
            dma((ny,)), dma((ny,)), dma((ny,)), dma((ny,)),
        ],
        compiler_params=pltpu.CompilerParams(collective_id=0, has_side_effects=True, vmem_limit_bytes=VMEM_LIMIT),
    )(inputs, master, factors)


def dot_t(a, b):
    return lax.dot_general(a, b, (((0,), (0,)), ((), ())), preferred_element_type=F32)


def dot_nt(a, b):
    return lax.dot_general(a, b, (((1,), (1,)), ((), ())), preferred_element_type=F32)


def inner_head(scale, tile, size, h, p_ref, g_ref, f_ref, acc):
    tokens = g_ref.shape[0]
    lane = pl.ds(pl.multiple_of(h * size, size), size)
    row = lax.broadcasted_iota(jnp.int32, (tile, tile), 0)
    col = lax.broadcasted_iota(jnp.int32, (tile, tile), 1)
    crossed = jnp.bitwise_xor(row, col)
    causal = row >= col
    for b in range(tokens // tile):
        span = slice(b * tile, (b + 1) * tile)
        queries, grads = p_ref[0, span, lane], g_ref[span, lane]
        weights = jnp.broadcast_to(f_ref[h, span, 0:1], (tile, tile))
        for level in range(1, LV_IN):
            factor = f_ref[h, span, level:level + 1]
            weights = jnp.where(crossed >= 1 << (level - 1), factor, weights)
        weights = jnp.where(causal, weights, 0.0)
        if b:
            rest = f_ref[h, span, LV_IN - 1:LV_IN]
            weights = jnp.concatenate([jnp.broadcast_to(rest, (tile, b * tile)), weights], axis=1)
        seen = slice(0, (b + 1) * tile)
        keys, values = p_ref[1, seen, lane], p_ref[2, seen, lane]
        probs = (scale * dot_nt(queries, keys) * weights).astype(BF16)
        mixed = (scale * dot_nt(grads, values) * weights).astype(BF16)
        acc[0, span, lane] = jnp.dot(probs, values, preferred_element_type=F32)
        acc[1, span, lane] = jnp.dot(mixed, keys, preferred_element_type=F32)
        to_keys = dot_t(mixed, queries)
        to_values = dot_t(probs, grads)
        if b:
            before = slice(0, b * tile)
            acc[2, before, lane] += to_keys[before]
            acc[3, before, lane] += to_values[before]
        acc[2, span, lane] = to_keys[b * tile:]
        acc[3, span, lane] = to_values[b * tile:]


def update_kernel(nz, nx, scale, depth, p_ref, g_ref, f_ref, xt_ref, m_ref, m1_ref, m2_ref, att_ref, out_ref,
                  acc, dy, sums, pend, sum_out, sum_in, pend_out, pend_in,
                  own, xsend, xrecv, zsend, zrecv, sse, rse, spe, rpe, ssx, rsx, ssz, rsz, sz, rz, sx, rx):
    rows = m_ref.shape[1]
    half = rows // 2
    heads = f_ref.shape[0]
    size = g_ref.shape[1] // heads
    tokens = g_ref.shape[0] * lax.axis_size("ctx")
    me = lax.axis_index("ctx")
    z, x = me // nx, me % nx
    gather = Gather(out_ref, nz, nx, rows, sz, rz, sx, rx)

    def partner(level):
        mask = 1 << level
        return {"ctx": me + mask - 2 * mask * (me // mask % 2)}

    greet(ctx_peers(nz, nx) + [partner(level) for level in range(depth)])
    started = []

    def state_copy(level):
        return pltpu.make_async_remote_copy(
            src_ref=sum_out.at[level], dst_ref=sum_in.at[level], send_sem=sse.at[level], recv_sem=rse.at[level],
            device_id=partner(level), device_id_type=MESH)

    def pend_copy(level):
        return pltpu.make_async_remote_copy(
            src_ref=pend_out.at[level, pl.ds(level, depth - level)],
            dst_ref=pend_in.at[level, pl.ds(level, depth - level)],
            send_sem=spe.at[level], recv_sem=rpe.at[level],
            device_id=partner(level), device_id_type=MESH)

    def state_start(level):
        sum_out[level] = sums[...].astype(BF16)
        state_copy(level).start()

    def state_end(level):
        state_copy(level).wait_recv()
        if level + 1 < depth:
            sums[...] += sum_in[level].astype(F32)
            state_start(level + 1)

    def pend_start(level):
        pend_out[level, level:] = pend[level:].astype(BF16)
        pend_copy(level).start()

    def pend_end(level):
        pend_copy(level).wait_recv()
        if level + 1 < depth:
            pend[level + 1:] += pend_in[level, level + 1:].astype(F32)
            pend_start(level + 1)

    @pl.loop(0, heads)
    def _(h):
        lane = pl.ds(pl.multiple_of(h * size, size), size)
        sums[h] = dot_t(p_ref[1, :, lane], p_ref[2, :, lane])

    state_start(0)

    @pl.loop(0, heads)
    def _(h):
        lane = pl.ds(pl.multiple_of(h * size, size), size)
        queries = p_ref[0, :, lane]
        grads = g_ref[:, lane].astype(F32)
        for level in range(depth):
            weighted = (f_ref[h, :, LV_IN + level:LV_IN + level + 1] * grads).astype(BF16)
            pend[level, h] = scale * dot_t(queries, weighted)

    pend_start(0)

    @pl.loop(0, heads)
    def _(h):
        inner_head(scale, min(256, g_ref.shape[0]), size, h, p_ref, g_ref, f_ref, acc)
        for level in range(depth):
            @pl.when(h == min(level, heads - 1))
            def _():
                state_end(level)
        for level in range(depth - 1):
            @pl.when(h == min(level + 2, heads - 1))
            def _():
                pend_end(level)

    @pl.loop(0, heads)
    def _(h):
        lane = pl.ds(pl.multiple_of(h * size, size), size)
        queries, grads = p_ref[0, :, lane], g_ref[:, lane]
        outer = jnp.zeros(queries.shape, F32)
        back = jnp.zeros(queries.shape, F32)
        for level in range(depth):
            factor = f_ref[h, :, LV_IN + level:LV_IN + level + 1]
            upper = jnp.full((size, size), (me >> level) & 1) == 1
            bucket = jnp.where(upper, sum_in[level, h].astype(F32), 0.0).astype(BF16)
            outer = outer + factor * jnp.dot(queries, bucket, preferred_element_type=F32)
            back = back + factor * dot_nt(grads, bucket)
        att_ref[:, lane] = (acc[0, :, lane] + scale * outer).astype(BF16)
        dy[0, :, lane] = (acc[1, :, lane] + scale * back).astype(BF16)

    def key_value_grads():
        @pl.loop(0, heads)
        def _(h):
            lane = pl.ds(pl.multiple_of(h * size, size), size)
            incoming = jnp.zeros((size, size), F32)
            for level in range(depth):
                lower = jnp.full((size, size), (me >> level) & 1) == 0
                incoming = incoming + jnp.where(lower, pend_in[level, level, h].astype(F32), 0.0)
            incoming = incoming.astype(BF16)
            dy[1, :, lane] = (acc[2, :, lane] + dot_nt(p_ref[2, :, lane], incoming)).astype(BF16)
            dy[2, :, lane] = (acc[3, :, lane] + jnp.dot(
                p_ref[1, :, lane], incoming, preferred_element_type=F32)).astype(BF16)

    def product(i, zb, xb):
        start = pl.multiple_of((zb * nx + xb) * rows, rows)
        return jnp.dot(xt_ref[pl.ds(start, rows), :], dy[i], preferred_element_type=F32)

    def x_copy(i, delta, p):
        return pltpu.make_async_remote_copy(
            src_ref=xsend.at[i, delta, p - 1], dst_ref=xrecv.at[i, delta, p - 1],
            send_sem=ssx.at[i, delta, p - 1], recv_sem=rsx.at[i, delta, p - 1],
            device_id={"ctx": z * nx + (x + p) % nx}, device_id_type=MESH)

    def z_copy(i, d, t):
        return pltpu.make_async_remote_copy(
            src_ref=zsend.at[i, d, t], dst_ref=zrecv.at[i, d, t],
            send_sem=ssz.at[i, d, t], recv_sem=rsz.at[i, d, t],
            device_id={"ctx": gather.ring_peer(d)}, device_id_type=MESH)

    order = []
    for k in range(1, nz // 2 + 1):
        order += [k] if k == nz - k else [k, nz - k]
    order.append(0)

    def side_partials(i):
        for delta in order:
            for p in range(1, nx):
                xsend[i, delta, p - 1] = product(i, (z + delta) % nz, (x + p) % nx).astype(BF16)
                started.append(x_copy(i, delta, p))
                started[-1].start()

    def own_partials(i):
        for delta in order:
            own[delta] = product(i, (z + delta) % nz, x)

    arrived = set()

    def reduce_step(i, d, t):
        delta = (nz - 1 - t) if d == 0 else (t + 1) % nz
        for p in range(1, nx):
            if (i, delta, p) not in arrived:
                arrived.add((i, delta, p))
                x_copy(i, delta, p).wait_recv()
        part = slice(d * half, (d + 1) * half)
        total = own[delta, part, :]
        for p in range(1, nx):
            total = total + xrecv[i, delta, p - 1, part, :].astype(F32)
        if t > 0:
            z_copy(i, d, t - 1).wait_recv()
            total = total + zrecv[i, d, t - 1].astype(F32)
        if t < nz - 1:
            zsend[i, d, t] = total.astype(BF16)
            started.append(z_copy(i, d, t))
            started[-1].start()
            return
        grad = total / tokens
        master = m_ref[i, part, :]
        first = 0.9 * m1_ref[i, part, :] + 0.1 * grad
        second = 0.95 * m2_ref[i, part, :] + 0.05 * grad * grad
        updated = master - 0.003 * (first / (jnp.sqrt(second) + 1e-08) + 0.1 * master)
        start = pl.multiple_of(me * rows + d * half, half)
        out_ref[i, pl.ds(start, half), :] = updated.astype(BF16)
        gather.send(i, d, 0)

    side_partials(0)
    pend_end(depth - 1)
    key_value_grads()
    side_partials(1)
    side_partials(2)
    for i in range(4):
        if i < 3:
            own_partials(i)
        for t in range(nz):
            for d in range(2):
                if i < 3:
                    reduce_step(i, d, t)
                if i > 0 and t < nz - 1:
                    gather.ring_step(i - 1, d, t)
    for i in range(3):
        gather.wait_side(i)
    gather.finish()
    for level in range(depth):
        started += [state_copy(level), pend_copy(level)]
    for copy in started:
        copy.wait_send()


def attend_and_update(projected, out_grad, factors, xt, master, moment_one, moment_two, nz, nx, scale, depth):
    rows, cols = master.shape[1:]
    heads, tokens = factors.shape[:2]
    size = cols // heads
    dma = pltpu.SemaphoreType.DMA
    vmem = pl.BlockSpec(memory_space=pltpu.VMEM)
    return pl.pallas_call(
        functools.partial(update_kernel, nz, nx, scale, depth),
        out_shape=(jax.ShapeDtypeStruct((tokens, cols), BF16), jax.ShapeDtypeStruct((3, xt.shape[0], cols), BF16)),
        in_specs=[vmem] * 7,
        out_specs=(vmem, vmem),
        scratch_shapes=[
            pltpu.VMEM((4, tokens, cols), F32),
            pltpu.VMEM((3, tokens, cols), BF16),
            pltpu.VMEM((heads, size, size), F32),
            pltpu.VMEM((depth, heads, size, size), F32),
            pltpu.VMEM((depth, heads, size, size), BF16),
            pltpu.VMEM((depth, heads, size, size), BF16),
            pltpu.VMEM((depth, depth, heads, size, size), BF16),
            pltpu.VMEM((depth, depth, heads, size, size), BF16),
            pltpu.VMEM((nz, rows, cols), F32),
            pltpu.VMEM((3, nz, nx - 1, rows, cols), BF16),
            pltpu.VMEM((3, nz, nx - 1, rows, cols), BF16),
            pltpu.VMEM((3, 2, nz - 1, rows // 2, cols), BF16),
            pltpu.VMEM((3, 2, nz - 1, rows // 2, cols), BF16),
            dma((depth,)), dma((depth,)), dma((depth,)), dma((depth,)),
            dma((3, nz, nx - 1)), dma((3, nz, nx - 1)),
            dma((3, 2, nz - 1)), dma((3, 2, nz - 1)),
            dma((3, 2, nz - 1, nx)), dma((3, 2, nz - 1, nx)),
            dma((3, 2, nz, nx - 1)), dma((3, 2, nz, nx - 1)),
        ],
        compiler_params=pltpu.CompilerParams(collective_id=1, has_side_effects=True, vmem_limit_bytes=VMEM_LIMIT),
    )(projected, out_grad, factors, xt, master, moment_one, moment_two)


def body(inputs, level_factors, out_grad, master, moment_one, moment_two):
    tokens_dev = inputs.shape[0]
    heads = level_factors.shape[0]
    head_size = out_grad.shape[1] // heads
    blocks = lax.axis_size("ctx")
    nz, nx = factor_ctx(blocks)
    depth = min(blocks.bit_length() - 1, level_factors.shape[1] - LV_IN)
    scale = 1.0 / math.sqrt(head_size * tokens_dev)
    projected, xt, factors = project(inputs, master, level_factors, nz, nx, lax.axis_size("head"))
    return attend_and_update(
        projected, out_grad, factors, xt, master, moment_one, moment_two, nz, nx, scale, depth)


def solution(mesh):
    placed = (
        P("ctx", "head"),
        P("head", None, "ctx"),
        P("ctx", "head"),
        P(None, "ctx", "head"),
        P(None, "ctx", "head"),
        P(None, "ctx", "head"),
    )
    return jax.shard_map(
        body,
        mesh=mesh,
        in_specs=placed,
        out_specs=(P("ctx", "head"), P(None, None, "head")),
        check_vma=False,
    )
```

```python
import functools
import math

import jax
import jax.numpy as jnp
from jax import lax
from jax.experimental import pallas as pl
from jax.experimental.pallas import tpu as pltpu
from jax.sharding import PartitionSpec as P

LV_IN = 8
MESH = pl.DeviceIdType.MESH
WIDE = ((1, 1),)
F32 = jnp.float32
BF16 = jnp.bfloat16
VMEM_LIMIT = 60 * 1024 * 1024


def factor_ctx(count):
    nx = 1 << ((count.bit_length() - 1) // 2)
    return count // nx, nx


class Gather:
    def __init__(self, ref, nz, nx, rows, sz, rz, sx, rx):
        self.ref, self.nz, self.nx, self.rows = ref, nz, nx, rows
        self.sz, self.rz, self.sx, self.rx = sz, rz, sx, rx
        me = lax.axis_index("ctx")
        self.z, self.x = me // nx, me % nx
        self.started = []

    def piece(self, i, d, z, x):
        half = self.rows // 2
        start = pl.multiple_of((z * self.nx + x) * self.rows + d * half, half)
        return self.ref.at[i, pl.ds(start, half), :]

    def origin(self, d, t):
        return (self.z + (self.nz - t if d == 0 else t)) % self.nz

    def ring_peer(self, d):
        return ((self.z + (1 if d == 0 else self.nz - 1)) % self.nz) * self.nx + self.x

    def ring_copy(self, i, d, s, z, q):
        view = self.piece(i, d, z, (self.x + q) % self.nx)
        return pltpu.make_async_remote_copy(
            src_ref=view, dst_ref=view, send_sem=self.sz.at[i, d, s, q], recv_sem=self.rz.at[i, d, s, q],
            device_id={"ctx": self.ring_peer(d)}, device_id_type=MESH)

    def side_copy(self, i, d, t, p, x):
        view = self.piece(i, d, self.origin(d, t), x)
        return pltpu.make_async_remote_copy(
            src_ref=view, dst_ref=view, send_sem=self.sx.at[i, d, t, p - 1], recv_sem=self.rx.at[i, d, t, p - 1],
            device_id={"ctx": self.z * self.nx + (self.x + p) % self.nx}, device_id_type=MESH)

    def start(self, copy):
        copy.start()
        self.started.append(copy)

    def send(self, i, d, t):
        if t < self.nz - 1:
            self.start(self.ring_copy(i, d, t, self.origin(d, t), 0))
        for p in range(1, self.nx):
            self.start(self.side_copy(i, d, t, p, self.x))

    def inject(self, i, d):
        for p in range(1, self.nx):
            self.side_copy(i, d, 0, p, (self.x + self.nx - p) % self.nx).wait_recv()
            self.start(self.ring_copy(i, d, 0, self.z, self.nx - p))

    def ring_step(self, i, d, s):
        wide = (i, d) in WIDE
        if wide and s == 0:
            self.inject(i, d)
        for q in range(self.nx if wide else 1):
            self.ring_copy(i, d, s, self.origin(d, s + 1), q).wait_recv()
            if wide and s + 1 < self.nz - 1:
                self.start(self.ring_copy(i, d, s + 1, self.origin(d, s + 1), q))
        if not wide:
            self.send(i, d, s + 1)

    def wait_side(self, i):
        for t in range(self.nz):
            for d in range(2):
                if (i, d) not in WIDE:
                    for p in range(1, self.nx):
                        self.side_copy(i, d, t, p, (self.x + self.nx - p) % self.nx).wait_recv()

    def finish(self):
        for copy in self.started:
            copy.wait_send()


def ctx_peers(nz, nx):
    me = lax.axis_index("ctx")
    z, x = me // nx, me % nx
    peers = [{"ctx": ((z + 1) % nz) * nx + x}, {"ctx": ((z + nz - 1) % nz) * nx + x}]
    peers += [{"ctx": z * nx + (x + p) % nx} for p in range(1, nx)]
    return peers


def greet(peers):
    barrier = pltpu.get_barrier_semaphore()
    for peer in peers:
        pl.semaphore_signal(barrier, inc=1, device_id=peer, device_id_type=MESH)
    pl.semaphore_wait(barrier, len(peers))


def project_kernel(nz, nx, nh, x_ref, m_ref, f_ref, p_ref, xt_ref, ft_ref, xs, ws, sz, rz, sx, rx, sy, ry, sc, rc):
    rows = m_ref.shape[1]
    width = x_ref.shape[1]
    ny = nh // 2
    head = lax.axis_index("head")
    y, core = head // 2, head % 2
    sibling = {"head": y * 2 + 1 - core}
    peers = ctx_peers(nz, nx) + [sibling]
    peers += [{"head": ((y + p) % ny) * 2 + core} for p in range(1, ny)]
    gather = Gather(ws, nz, nx, rows, sz, rz, sx, rx)
    own = pl.multiple_of(lax.axis_index("ctx") * rows, rows)
    for i in range(3):
        ws[i, pl.ds(own, rows), :] = m_ref[i].astype(BF16)

    def columns(h):
        return xs.at[:, pl.ds(pl.multiple_of(h * width, width), width)]

    greet(peers)
    xs[:, pl.ds(pl.multiple_of(head * width, width), width)] = x_ref[...]
    started = []

    def y_copy(p, h):
        return pltpu.make_async_remote_copy(
            src_ref=columns(h), dst_ref=columns(h), send_sem=sy.at[p], recv_sem=ry.at[p],
            device_id={"head": ((y + p) % ny) * 2 + core}, device_id_type=MESH)

    def core_copy(p, h):
        return pltpu.make_async_remote_copy(
            src_ref=columns(h), dst_ref=columns(h), send_sem=sc.at[p], recv_sem=rc.at[p],
            device_id=sibling, device_id_type=MESH)

    for i in range(3):
        for d in range(2):
            gather.send(i, d, 0)
        if i == 0:
            for p in range(1, ny):
                started.append(y_copy(p, head))
                started[-1].start()
            started.append(core_copy(0, head))
            started[-1].start()

    def ring(i):
        for s in range(nz - 1):
            for d in range(2):
                gather.ring_step(i, d, s)

    def dots(i):
        tile = min(512, xs.shape[0])

        @pl.loop(0, xs.shape[0] // tile)
        def _(r):
            span = pl.ds(pl.multiple_of(r * tile, tile), tile)
            p_ref[i, span, :] = jnp.dot(xs[span, :], ws[i], preferred_element_type=F32).astype(BF16)

    for h in range(f_ref.shape[0]):
        ft_ref[h] = f_ref[h].T
    ring(0)
    for p in range(1, ny):
        source = ((y + ny - p) % ny) * 2 + core
        y_copy(p, source).wait_recv()
        started.append(core_copy(p, source))
        started[-1].start()
    ring(1)
    for p in range(ny):
        core_copy(p, ((y + ny - p) % ny) * 2 + 1 - core).wait_recv()
    piece = min(256, width)

    @pl.loop(0, xs.shape[1] // piece)
    def _(r):
        span = pl.ds(pl.multiple_of(r * piece, piece), piece)
        xt_ref[span, :] = xs[:, span].T

    gather.wait_side(0)
    dots(0)
    ring(2)
    for i in range(1, 3):
        gather.wait_side(i)
        dots(i)
    gather.finish()
    for copy in started:
        copy.wait_send()


def project(inputs, master, factors, nz, nx, nh):
    tokens, width = inputs.shape
    rows, cols = master.shape[1:]
    features = width * nh
    dma = pltpu.SemaphoreType.DMA
    ny = nh // 2
    vmem = pl.BlockSpec(memory_space=pltpu.VMEM)
    return pl.pallas_call(
        functools.partial(project_kernel, nz, nx, nh),
        out_shape=(jax.ShapeDtypeStruct((3, tokens, cols), BF16), jax.ShapeDtypeStruct((features, tokens), BF16),
                   jax.ShapeDtypeStruct((factors.shape[0], tokens, factors.shape[1]), F32)),
        in_specs=[vmem] * 3,
        out_specs=(vmem,) * 3,
        scratch_shapes=[
            pltpu.VMEM((tokens, features), BF16),
            pltpu.VMEM((3, features, cols), BF16),
            dma((3, 2, nz - 1, nx)), dma((3, 2, nz - 1, nx)),
            dma((3, 2, nz, nx - 1)), dma((3, 2, nz, nx - 1)),
            dma((ny,)), dma((ny,)), dma((ny,)), dma((ny,)),
        ],
        compiler_params=pltpu.CompilerParams(collective_id=0, has_side_effects=True, vmem_limit_bytes=VMEM_LIMIT),
    )(inputs, master, factors)


def dot_t(a, b):
    return lax.dot_general(a, b, (((0,), (0,)), ((), ())), preferred_element_type=F32)


def dot_nt(a, b):
    return lax.dot_general(a, b, (((1,), (1,)), ((), ())), preferred_element_type=F32)


def inner_head(scale, tile, size, h, p_ref, g_ref, f_ref, acc):
    tokens = g_ref.shape[0]
    lane = pl.ds(pl.multiple_of(h * size, size), size)
    row = lax.broadcasted_iota(jnp.int32, (tile, tile), 0)
    col = lax.broadcasted_iota(jnp.int32, (tile, tile), 1)
    crossed = jnp.bitwise_xor(row, col)
    causal = row >= col
    for b in range(tokens // tile):
        span = slice(b * tile, (b + 1) * tile)
        queries, grads = p_ref[0, span, lane], g_ref[span, lane]
        weights = jnp.broadcast_to(f_ref[h, span, 0:1], (tile, tile))
        for level in range(1, LV_IN):
            factor = f_ref[h, span, level:level + 1]
            weights = jnp.where(crossed >= 1 << (level - 1), factor, weights)
        weights = jnp.where(causal, weights, 0.0)
        if b:
            rest = f_ref[h, span, LV_IN - 1:LV_IN]
            weights = jnp.concatenate([jnp.broadcast_to(rest, (tile, b * tile)), weights], axis=1)
        seen = slice(0, (b + 1) * tile)
        keys, values = p_ref[1, seen, lane], p_ref[2, seen, lane]
        probs = (scale * dot_nt(queries, keys) * weights).astype(BF16)
        mixed = (scale * dot_nt(grads, values) * weights).astype(BF16)
        acc[0, span, lane] = jnp.dot(probs, values, preferred_element_type=F32)
        acc[1, span, lane] = jnp.dot(mixed, keys, preferred_element_type=F32)
        to_keys = dot_t(mixed, queries)
        to_values = dot_t(probs, grads)
        if b:
            before = slice(0, b * tile)
            acc[2, before, lane] += to_keys[before]
            acc[3, before, lane] += to_values[before]
        acc[2, span, lane] = to_keys[b * tile:]
        acc[3, span, lane] = to_values[b * tile:]


def update_kernel(nz, nx, scale, depth, p_ref, g_ref, f_ref, xt_ref, m_ref, m1_ref, m2_ref, att_ref, out_ref,
                  acc, dy, sums, pend, sum_out, sum_in, top_out, top_in, pend_out, pend_in,
                  own, xsend, xrecv, zsend, zrecv, sse, rse, spe, rpe, ssx, rsx, ssz, rsz, sz, rz, sx, rx):
    rows = m_ref.shape[1]
    half = rows // 2
    heads = f_ref.shape[0]
    size = g_ref.shape[1] // heads
    tokens = g_ref.shape[0] * lax.axis_size("ctx")
    me = lax.axis_index("ctx")
    z, x = me // nx, me % nx
    gather = Gather(out_ref, nz, nx, rows, sz, rz, sx, rx)

    def partner(level):
        mask = 1 << level
        return {"ctx": me + mask - 2 * mask * (me // mask % 2)}

    greet(ctx_peers(nz, nx) + [partner(level) for level in range(depth)])
    started = []

    def state_copy(level):
        last = level == depth - 1
        return pltpu.make_async_remote_copy(
            src_ref=top_out if last else sum_out.at[level], dst_ref=top_in if last else sum_in.at[level],
            send_sem=sse.at[level], recv_sem=rse.at[level],
            device_id=partner(level), device_id_type=MESH)

    def pend_copy(level):
        return pltpu.make_async_remote_copy(
            src_ref=pend_out.at[level, pl.ds(level, depth - level)],
            dst_ref=pend_in.at[level, pl.ds(level, depth - level)],
            send_sem=spe.at[level], recv_sem=rpe.at[level],
            device_id=partner(level), device_id_type=MESH)

    def state_start(level):
        if level < depth - 1:
            sum_out[level] = sums[...]
        else:
            top_out[...] = sums[...].astype(BF16)
        state_copy(level).start()

    def state_end(level):
        state_copy(level).wait_recv()
        if level + 1 < depth:
            sums[...] += sum_in[level]
            state_start(level + 1)

    def pend_start(level):
        pend_out[level, level:] = pend[level:].astype(BF16)
        pend_copy(level).start()

    def pend_end(level):
        pend_copy(level).wait_recv()
        if level + 1 < depth:
            pend[level + 1:] += pend_in[level, level + 1:].astype(F32)
            pend_start(level + 1)

    @pl.loop(0, heads)
    def _(h):
        lane = pl.ds(pl.multiple_of(h * size, size), size)
        sums[h] = dot_t(p_ref[1, :, lane], p_ref[2, :, lane])

    state_start(0)

    @pl.loop(0, heads)
    def _(h):
        lane = pl.ds(pl.multiple_of(h * size, size), size)
        queries = p_ref[0, :, lane]
        grads = g_ref[:, lane].astype(F32)
        for level in range(depth):
            weighted = (f_ref[h, :, LV_IN + level:LV_IN + level + 1] * grads).astype(BF16)
            pend[level, h] = scale * dot_t(queries, weighted)

    pend_start(0)

    @pl.loop(0, heads)
    def _(h):
        inner_head(scale, min(256, g_ref.shape[0]), size, h, p_ref, g_ref, f_ref, acc)
        for level in range(depth):
            @pl.when(h == min(level, heads - 1))
            def _():
                state_end(level)
        for level in range(depth - 1):
            @pl.when(h == min(level + 2, heads - 1))
            def _():
                pend_end(level)

    @pl.loop(0, heads)
    def _(h):
        lane = pl.ds(pl.multiple_of(h * size, size), size)
        queries, grads = p_ref[0, :, lane], g_ref[:, lane]
        outer = jnp.zeros(queries.shape, F32)
        back = jnp.zeros(queries.shape, F32)
        for level in range(depth):
            factor = f_ref[h, :, LV_IN + level:LV_IN + level + 1]
            upper = jnp.full((size, size), (me >> level) & 1) == 1
            sent = sum_in[level, h] if level < depth - 1 else top_in[h].astype(F32)
            bucket = jnp.where(upper, sent, 0.0).astype(BF16)
            outer = outer + factor * jnp.dot(queries, bucket, preferred_element_type=F32)
            back = back + factor * dot_nt(grads, bucket)
        att_ref[:, lane] = (acc[0, :, lane] + scale * outer).astype(BF16)
        dy[0, :, lane] = (acc[1, :, lane] + scale * back).astype(BF16)

    def key_value_grads():
        @pl.loop(0, heads)
        def _(h):
            lane = pl.ds(pl.multiple_of(h * size, size), size)
            incoming = jnp.zeros((size, size), F32)
            for level in range(depth):
                lower = jnp.full((size, size), (me >> level) & 1) == 0
                incoming = incoming + jnp.where(lower, pend_in[level, level, h].astype(F32), 0.0)
            incoming = incoming.astype(BF16)
            dy[1, :, lane] = (acc[2, :, lane] + dot_nt(p_ref[2, :, lane], incoming)).astype(BF16)
            dy[2, :, lane] = (acc[3, :, lane] + jnp.dot(
                p_ref[1, :, lane], incoming, preferred_element_type=F32)).astype(BF16)

    def product(i, zb, xb):
        start = pl.multiple_of((zb * nx + xb) * rows, rows)
        return jnp.dot(xt_ref[pl.ds(start, rows), :], dy[i], preferred_element_type=F32)

    def x_copy(i, delta, p):
        return pltpu.make_async_remote_copy(
            src_ref=xsend.at[i, delta, p - 1], dst_ref=xrecv.at[i, delta, p - 1],
            send_sem=ssx.at[i, delta, p - 1], recv_sem=rsx.at[i, delta, p - 1],
            device_id={"ctx": z * nx + (x + p) % nx}, device_id_type=MESH)

    def z_copy(i, d, t):
        return pltpu.make_async_remote_copy(
            src_ref=zsend.at[i, d, t], dst_ref=zrecv.at[i, d, t],
            send_sem=ssz.at[i, d, t], recv_sem=rsz.at[i, d, t],
            device_id={"ctx": gather.ring_peer(d)}, device_id_type=MESH)

    order = []
    for k in range(1, nz // 2 + 1):
        order += [k] if k == nz - k else [k, nz - k]
    order.append(0)

    def side_partials(i):
        for delta in order:
            for p in range(1, nx):
                xsend[i, delta, p - 1] = product(i, (z + delta) % nz, (x + p) % nx).astype(BF16)
                started.append(x_copy(i, delta, p))
                started[-1].start()

    def own_partials(i):
        for delta in order:
            own[delta] = product(i, (z + delta) % nz, x)

    arrived = set()

    def reduce_step(i, d, t):
        delta = (nz - 1 - t) if d == 0 else (t + 1) % nz
        for p in range(1, nx):
            if (i, delta, p) not in arrived:
                arrived.add((i, delta, p))
                x_copy(i, delta, p).wait_recv()
        part = slice(d * half, (d + 1) * half)
        total = own[delta, part, :]
        for p in range(1, nx):
            total = total + xrecv[i, delta, p - 1, part, :].astype(F32)
        if t > 0:
            z_copy(i, d, t - 1).wait_recv()
            total = total + zrecv[i, d, t - 1].astype(F32)
        if t < nz - 1:
            zsend[i, d, t] = total.astype(BF16)
            started.append(z_copy(i, d, t))
            started[-1].start()
            return
        grad = total / tokens
        master = m_ref[i, part, :]
        first = 0.9 * m1_ref[i, part, :] + 0.1 * grad
        second = 0.95 * m2_ref[i, part, :] + 0.05 * grad * grad
        updated = master - 0.003 * (first / (jnp.sqrt(second) + 1e-08) + 0.1 * master)
        start = pl.multiple_of(me * rows + d * half, half)
        out_ref[i, pl.ds(start, half), :] = updated.astype(BF16)
        gather.send(i, d, 0)

    side_partials(0)
    pend_end(depth - 1)
    key_value_grads()
    side_partials(1)
    side_partials(2)
    for i in range(4):
        if i < 3:
            own_partials(i)
        for t in range(nz):
            for d in range(2):
                if i < 3:
                    reduce_step(i, d, t)
                if i > 0 and t < nz - 1:
                    gather.ring_step(i - 1, d, t)
    for i in range(3):
        gather.wait_side(i)
    gather.finish()
    for level in range(depth):
        started += [state_copy(level), pend_copy(level)]
    for copy in started:
        copy.wait_send()


def attend_and_update(projected, out_grad, factors, xt, master, moment_one, moment_two, nz, nx, scale, depth):
    rows, cols = master.shape[1:]
    heads, tokens = factors.shape[:2]
    size = cols // heads
    dma = pltpu.SemaphoreType.DMA
    vmem = pl.BlockSpec(memory_space=pltpu.VMEM)
    return pl.pallas_call(
        functools.partial(update_kernel, nz, nx, scale, depth),
        out_shape=(jax.ShapeDtypeStruct((tokens, cols), BF16), jax.ShapeDtypeStruct((3, xt.shape[0], cols), BF16)),
        in_specs=[vmem] * 7,
        out_specs=(vmem, vmem),
        scratch_shapes=[
            pltpu.VMEM((4, tokens, cols), F32),
            pltpu.VMEM((3, tokens, cols), BF16),
            pltpu.VMEM((heads, size, size), F32),
            pltpu.VMEM((depth, heads, size, size), F32),
            pltpu.VMEM((depth, heads, size, size), F32),
            pltpu.VMEM((depth, heads, size, size), F32),
            pltpu.VMEM((heads, size, size), BF16),
            pltpu.VMEM((heads, size, size), BF16),
            pltpu.VMEM((depth, depth, heads, size, size), BF16),
            pltpu.VMEM((depth, depth, heads, size, size), BF16),
            pltpu.VMEM((nz, rows, cols), F32),
            pltpu.VMEM((3, nz, nx - 1, rows, cols), BF16),
            pltpu.VMEM((3, nz, nx - 1, rows, cols), BF16),
            pltpu.VMEM((3, 2, nz - 1, rows // 2, cols), BF16),
            pltpu.VMEM((3, 2, nz - 1, rows // 2, cols), BF16),
            dma((depth,)), dma((depth,)), dma((depth,)), dma((depth,)),
            dma((3, nz, nx - 1)), dma((3, nz, nx - 1)),
            dma((3, 2, nz - 1)), dma((3, 2, nz - 1)),
            dma((3, 2, nz - 1, nx)), dma((3, 2, nz - 1, nx)),
            dma((3, 2, nz, nx - 1)), dma((3, 2, nz, nx - 1)),
        ],
        compiler_params=pltpu.CompilerParams(collective_id=1, has_side_effects=True, vmem_limit_bytes=VMEM_LIMIT),
    )(projected, out_grad, factors, xt, master, moment_one, moment_two)


def body(inputs, level_factors, out_grad, master, moment_one, moment_two):
    tokens_dev = inputs.shape[0]
    heads = level_factors.shape[0]
    head_size = out_grad.shape[1] // heads
    blocks = lax.axis_size("ctx")
    nz, nx = factor_ctx(blocks)
    depth = min(blocks.bit_length() - 1, level_factors.shape[1] - LV_IN)
    scale = 1.0 / math.sqrt(head_size * tokens_dev)
    projected, xt, factors = project(inputs, master, level_factors, nz, nx, lax.axis_size("head"))
    return attend_and_update(
        projected, out_grad, factors, xt, master, moment_one, moment_two, nz, nx, scale, depth)


def solution(mesh):
    placed = (
        P("ctx", "head"),
        P("head", None, "ctx"),
        P("ctx", "head"),
        P(None, "ctx", "head"),
        P(None, "ctx", "head"),
        P(None, "ctx", "head"),
    )
    return jax.shard_map(
        body,
        mesh=mesh,
        in_specs=placed,
        out_specs=(P("ctx", "head"), P(None, None, "head")),
        check_vma=False,
    )
```
